32 devices in a mesh: leaf: 8 (over z, x), vec: 4 (over y, core).
Axes of the slice: x: 2, y: 2, z: 4, core: 2. Of those that a mesh axis runs over, the one named last changes fastest.
Arguments:
- vectors: bfloat16 [16384, 512], P('leaf', 'vec'), may hold values from -6 to 6
- leaf_basis: bfloat16 [32, 512, 256], P('leaf'), may hold values from -0.25 to 0.25
- up_leaf: bfloat16 [32, 256, 256], P('leaf'), may hold values from -0.25 to 0.25
- up_mid: bfloat16 [16, 256, 256], P('leaf'), may hold values from -0.25 to 0.25
- top_up: bfloat16 [8, 256, 256], P('leaf'), may hold values from -0.125 to 0.125
- top_down: bfloat16 [8, 256, 256], P('leaf'), may hold values from -0.375 to 0.375
- couplings: bfloat16 [16, 256, 256], replicated, may hold values from -0.125 to 0.125
- coupling_top: bfloat16 [256, 256], replicated, may hold values from -0.375 to 0.375
- near_blocks: bfloat16 [32, 5, 512, 512], P('leaf', None, 'vec'), may hold values from -0.125 to 0.125
- far_owner: int32 [448, 1], replicated, may hold values from 0 to 7; in each aligned block of 56 rows (0 to 55, 56 to 111, ...) at most 9 rows name the same one
- far_pick: int32 [448], replicated, may hold values from 0 to 3
- far_kind: int32 [448], P('leaf'), may hold values from 0 to 15
Outputs:
- result: bfloat16 [16384, 512], P('leaf', 'vec')
The draws below stay inside these ranges and needn't reach their ends.
Inputs may be any that keep to these rules, and one draw needn't show every extreme that they name: `far_owner`: among the 56 rows r of one aligned block (the far pairs of one subtree), no subtree is named more than 9 times, and in every draw some block names some subtree exactly 9 times.
All inputs are finite; a program needn't handle non-finite values.
Results may differ from the reference program's by a relative error of at most 0.009.
Values may be sent and summed in bfloat16 or wider, within the bound.
A program may use at most 128 MiB of HBM per device.

```python
import math
import jax
import jax.numpy as jnp
import numpy as np
from jax import lax

LEAF = 512
RANK = 256
NV = 512
KINDS = 16
NEAR = 5
FAR_LEAF = 8
FAR_MID = 8
FAR_ROOT = 8
LEAVES = 32
MIDS = 16
ROWS = 16384
FAR_DEV = 56
CAP = 9
N_LEAF = 8


def touch_ends(result, own_key, least, high):
    index_at = [jax.random.randint(jax.random.fold_in(own_key, axis), (), 0, length) for axis, length in enumerate(result.shape)]
    widest = result.shape.index(max(result.shape))
    next_to = index_at[:widest] + [(index_at[widest] + 1) % result.shape[widest]] + index_at[widest + 1:]
    return result.at[tuple(index_at)].set(least).at[tuple(next_to)].set(high)


def shard_levels(key, shape, cuts, least, largest):
    level, own = 1.0, jax.random.fold_in(key, 6)
    for axis_at, parts in cuts:
        heights = jnp.exp(jax.random.uniform(jax.random.fold_in(own, axis_at), (parts,), jnp.float32, least / len(cuts), largest / len(cuts)))
        level = level * jnp.repeat(heights, shape[axis_at] // parts).reshape([-1 if axis == axis_at else 1 for axis in range(len(shape))])
    return level


def deal_out(rng, own, number, rows, amount, top, most, lean):
    sequence = jax.random.permutation(rng, amount)
    crowded, common = load_shares(amount, rows * top, most, lean, True), load_shares(amount, rows * top, most, lean, False)
    places = jnp.arange(amount)

    def named(lengths, turn):
        used = int((lengths > 0).sum())
        fixed = max(1, used // 4)
        moved = fixed + (places - fixed + turn * (used - fixed)) % max(1, amount - fixed)
        return jnp.zeros((amount,), jnp.int32).at[sequence[jnp.where(places < fixed, places, moved)]].set(jnp.asarray(lengths, jnp.int32))

    lengths = jnp.where(number % 4 == 0, named(crowded, number // 4), named(common, number - number // 4 - 1))
    mixed = jax.random.permutation(jax.random.fold_in(own, 3), amount)
    donor, receiver = mixed[0:amount // 2 * 2:2], mixed[1:amount // 2 * 2:2]
    margin = jnp.minimum(lengths[donor] - 1, most - lengths[receiver]) // 2
    margin = jnp.where((donor == sequence[0]) | (receiver == sequence[0]) | (lengths[receiver] == 0), 0, jnp.maximum(margin, 0))
    moved = jax.random.randint(jax.random.fold_in(own, 4), (amount // 2,), 0, 1 << 20) % (margin + 1)
    lengths = lengths.at[donor].add(-moved).at[receiver].add(moved)
    members = jnp.searchsorted(jnp.cumsum(lengths), jnp.arange(rows * top), side="right").astype(jnp.int32)
    grid = members.reshape(top, rows).T
    grid = grid[jax.random.permutation(jax.random.fold_in(own, 1), rows)]
    turn = jax.random.randint(jax.random.fold_in(own, 2), (rows, 1), 0, top)
    return jnp.take_along_axis(grid, (jnp.arange(top)[None, :] + turn) % top, axis=1)


def load_shares(count, total, limit, lean, full):
    portions = [(1 << 20) // math.isqrt(standing ** lean) + 1 for standing in range(1, count + 1)]
    largest = limit if full else min(limit, max(-(-total // count), total * portions[0] // sum(portions)))
    least = 1 if total - largest >= count - 1 else 0
    given, rest = [largest] + [least] * (count - 1), total - largest - least * (count - 1)
    while rest > 0:
        candidates = [i for i in range(1, count) if given[i] < largest] or [i for i in range(1, count) if given[i] < limit]
        whole, remaining = sum([portions[i] for i in candidates]), rest
        for i in candidates:
            extra = min(limit - given[i], max(1, remaining * portions[i] // whole), rest)
            given[i] = given[i] + extra
            rest = rest - extra
    return np.array(given)


def noise(key, shape, deviation, limit, shards=(), held_as=jnp.bfloat16):
    drawn = jax.random.normal(key, shape, jnp.float32) * deviation
    if len(shards) > 0:
        drawn = shard_levels(key, shape, shards, -0.22, 0.18) * drawn
    return jnp.clip(drawn, min=-limit, max=limit).astype(held_as)


def setup_inputs(seed: int = 0) -> dict:
    keys = jax.random.split(jax.random.key(seed), 13)
    vectors = noise(keys[0], (ROWS, NV), 1.0, 6.0, ((0, 8), (1, 4)))
    leaf_basis = noise(keys[1], (LEAVES, LEAF, RANK), LEAF ** -0.5, 0.25, ((0, 8),))
    up_leaf = noise(keys[2], (LEAVES, RANK, RANK), (2 * RANK) ** -0.5, 0.25, ((0, 8),))
    up_mid = noise(keys[3], (MIDS, RANK, RANK), (2 * RANK) ** -0.5, 0.25, ((0, 8),))
    top_up = noise(keys[4], (N_LEAF, RANK, RANK), (RANK * N_LEAF) ** -0.5, 0.125, ((0, 8),))
    top_down = noise(keys[5], (N_LEAF, RANK, RANK), RANK ** -0.5, 0.375, ((0, 8),))
    couplings = noise(keys[6], (KINDS, RANK, RANK), (RANK * FAR_LEAF) ** -0.5, 0.125)
    coupling_top = noise(keys[7], (RANK, RANK), RANK ** -0.5, 0.375)
    near_blocks = noise(keys[8], (LEAVES, NEAR, LEAF, LEAF), (LEAF * NEAR) ** -0.5, 0.125, ((0, 8), (2, 4)))
    far_owner_keys = jax.random.split(jax.random.fold_in(keys[9], 1), (N_LEAF * FAR_DEV) // FAR_DEV)
    far_owner_turns = jax.random.permutation(jax.random.fold_in(keys[9], 3), (N_LEAF * FAR_DEV) // FAR_DEV)
    far_owner = jax.vmap(lambda own, number: deal_out(jax.random.fold_in(keys[9], 2), own, number, FAR_DEV, N_LEAF, 1, CAP, 1))(far_owner_keys, far_owner_turns).reshape((N_LEAF * FAR_DEV, 1))
    far_pick = touch_ends(jax.random.randint(keys[10], (N_LEAF * FAR_DEV,), 0, 4), jax.random.fold_in(keys[10], 1), 0, 3).astype(jnp.int32)
    far_kind = touch_ends(jax.random.randint(keys[11], (N_LEAF * FAR_DEV,), 0, KINDS), jax.random.fold_in(keys[11], 1), 0, KINDS - 1).astype(jnp.int32)
    return dict(vectors=vectors, leaf_basis=leaf_basis, up_leaf=up_leaf, up_mid=up_mid, top_up=top_up, top_down=top_down, couplings=couplings, coupling_top=coupling_top, near_blocks=near_blocks, far_owner=far_owner, far_pick=far_pick, far_kind=far_kind)


def couple(packed, coeff_leaf, coeff_mid, coeff_root, couplings):
    owners, pick_ids, kind_ids = packed
    first_end = 4 * FAR_LEAF
    second_end = first_end + 2 * FAR_MID
    source_leaf = owners[:first_end] * 4 + pick_ids[:first_end] % 4
    source_mid = owners[first_end:second_end] * 2 + pick_ids[first_end:second_end] % 2
    source_root = owners[second_end:]
    partner_coeffs = jnp.concatenate([jnp.take(coeff_leaf, source_leaf, axis=0), jnp.take(coeff_mid, source_mid, axis=0), jnp.take(coeff_root, source_root, axis=0)], axis=0).astype(jnp.float32)
    matrices = jnp.take(couplings, kind_ids, axis=0).astype(jnp.float32)
    products = jnp.einsum('frs,fsv->frv', matrices, partner_coeffs)
    far_leaf = products[:first_end].reshape(4, FAR_LEAF, RANK, NV).sum(axis=1)
    far_mid = products[first_end:second_end].reshape(2, FAR_MID, RANK, NV).sum(axis=1)
    far_root = products[second_end:].reshape(1, FAR_ROOT, RANK, NV).sum(axis=1)
    return far_leaf, far_mid, far_root


def reference(vectors, leaf_basis, up_leaf, up_mid, top_up, top_down, couplings, coupling_top, near_blocks, far_owner, far_pick, far_kind):
    blocked = vectors.reshape(LEAVES, LEAF, NV).astype(jnp.float32)
    coeff_leaf = jnp.einsum('nlr,nlv->nrv', leaf_basis.astype(jnp.float32), blocked).astype(jnp.bfloat16)
    coeff_mid = jnp.einsum('nrs,nrv->nsv', up_leaf.astype(jnp.float32), coeff_leaf.astype(jnp.float32)).reshape(MIDS, 2, RANK, NV).sum(axis=1).astype(jnp.bfloat16)
    coeff_root = jnp.einsum('nrs,nrv->nsv', up_mid.astype(jnp.float32), coeff_mid.astype(jnp.float32)).reshape(N_LEAF, 2, RANK, NV).sum(axis=1).astype(jnp.bfloat16)
    top_coeff = jnp.einsum('nrs,nrv->sv', top_up.astype(jnp.float32), coeff_root.astype(jnp.float32)).astype(jnp.bfloat16)
    top_local = jnp.dot(coupling_top, top_coeff, preferred_element_type=jnp.float32).astype(jnp.bfloat16)
    top_share = jnp.einsum('nrs,sv->nrv', top_down.astype(jnp.float32), top_local.astype(jnp.float32))
    packed = (far_owner.reshape(N_LEAF, FAR_DEV), far_pick.reshape(N_LEAF, FAR_DEV), far_kind.reshape(N_LEAF, FAR_DEV))
    far_leaf, far_mid, far_root = lax.map(lambda item: couple(item, coeff_leaf, coeff_mid, coeff_root, couplings), packed)
    far_leaf = far_leaf.reshape(LEAVES, RANK, NV)
    far_mid = far_mid.reshape(MIDS, RANK, NV)
    far_root = far_root.reshape(N_LEAF, RANK, NV)
    down_root = (far_root + top_share).astype(jnp.bfloat16)
    down_mid = (far_mid + jnp.einsum('nrs,nsv->nrv', up_mid.astype(jnp.float32), jnp.repeat(down_root, 2, axis=0).astype(jnp.float32))).astype(jnp.bfloat16)
    down_leaf = (far_leaf + jnp.einsum('nrs,nsv->nrv', up_leaf.astype(jnp.float32), jnp.repeat(down_mid, 2, axis=0).astype(jnp.float32))).astype(jnp.bfloat16)
    far_field = jnp.einsum('nlr,nrv->nlv', leaf_basis.astype(jnp.float32), down_leaf.astype(jnp.float32))
    halo_rows = (NEAR // 2) * LEAF
    padded = jnp.pad(vectors.astype(jnp.float32), ((halo_rows, halo_rows), (0, 0)))
    near_field = jnp.zeros((LEAVES, LEAF, NV), jnp.float32)
    for offset in range(NEAR):
        window = padded[offset * LEAF: offset * LEAF + ROWS].reshape(LEAVES, LEAF, NV)
        near_field = near_field + jnp.einsum('nil,nlv->niv', near_blocks[:, offset].astype(jnp.float32), window)
    return (far_field + near_field).reshape(ROWS, NV).astype(jnp.bfloat16)
```

```python
import functools
import jax
import jax.numpy as jnp
import numpy as np
from jax import lax
from jax.experimental import pallas as pl
from jax.experimental.pallas import tpu as pltpu
from jax.sharding import PartitionSpec as P

LEAF = 512
RANK = 256
NEAR = 5
FAR_LEAF = 8
FAR_MID = 8
FAR_ROOT = 8
HALO = NEAR // 2
CHUNK = 4
F32 = jnp.float32
BF16 = jnp.bfloat16


def dot(a, b):
    return jnp.dot(a, b, preferred_element_type=F32)


def dot_t(a, b):
    return lax.dot_general(a, b, (((0,), (0,)), ((), ())), preferred_element_type=F32)


def ring_position(leaf, count):
    return jnp.where(leaf % 2 == 1, leaf // 2, count - 1 - leaf // 2)


def leaf_at(position, count):
    half = count // 2
    return jnp.where(position < half, 2 * position + 1, 2 * (count - 1 - position))


def kernel(
    n,
    w,
    slot_ref,
    kind_ref,
    vec_hbm,
    basis_hbm,
    up_leaf_hbm,
    up_mid_hbm,
    top_up_hbm,
    top_down_hbm,
    coup_hbm,
    coup_top_hbm,
    near_hbm,
    out_ref,
    vecs,
    basis,
    up_leaf,
    up_mid,
    top_up,
    top_down,
    coup,
    coup_top,
    near,
    low_coeffs,
    high_coeffs,
    acc,
    far,
    near_out,
    near_in,
    local_sem,
    halo_send,
    halo_recv,
    vec_send,
    vec_recv,
    ring_send,
    ring_recv,
    back_send,
    back_recv,
):
    span = vec_hbm.shape[0]
    leaves = span // LEAF
    rows = near.shape[2]
    width = vec_hbm.shape[1]
    halo = HALO * LEAF
    me = lax.axis_index("leaf")
    mv = lax.axis_index("vec")
    pos = ring_position(me, n)
    nxt = leaf_at((pos + 1) % n, n)
    prv = leaf_at((pos + n - 1) % n, n)
    core, high = mv % 2, mv // 2
    highs = w // 2
    buddy = high * 2 + 1 - core

    def at(leaf=None, vec=None):
        return (me if leaf is None else leaf, mv if vec is None else vec)

    locals_ = [
        (vec_hbm, vecs.at[mv, pl.ds(halo, span)]),
        (basis_hbm, basis),
        (up_leaf_hbm, up_leaf),
        (up_mid_hbm, up_mid),
        (top_up_hbm, top_up),
        (near_hbm, near),
        (coup_hbm, coup),
        (top_down_hbm, top_down),
        (coup_top_hbm, coup_top),
    ]
    loads = [
        pltpu.make_async_copy(src, dst, local_sem.at[k]) for k, (src, dst) in enumerate(locals_)
    ]
    for load in loads:
        load.start()

    barrier = pltpu.get_barrier_semaphore()

    def greet(device):
        pl.semaphore_signal(barrier, inc=1, device_id=device, device_id_type=pl.DeviceIdType.MESH)

    greet(at(leaf=nxt))
    greet(at(leaf=prv))
    for d in range(1, w):
        greet(at(vec=(mv + d) % w))

    @pl.when(me > 0)
    def _():
        greet(at(leaf=me - 1))

    @pl.when(me < n - 1)
    def _():
        greet(at(leaf=me + 1))

    pl.semaphore_wait(
        barrier, w + 1 + (me > 0).astype(jnp.int32) + (me < n - 1).astype(jnp.int32)
    )

    def remote(src, dst, send, recv, device):
        return pltpu.make_async_remote_copy(
            src_ref=src,
            dst_ref=dst,
            send_sem=send,
            recv_sem=recv,
            device_id=device,
            device_id_type=pl.DeviceIdType.MESH,
        )

    def halo_copy(side):
        if side == 0:
            src = vec_hbm.at[pl.ds(span - halo, halo)]
            dst = vecs.at[mv, pl.ds(0, halo)]
            to = at(leaf=me + 1)
        else:
            src = vec_hbm.at[pl.ds(0, halo)]
            dst = vecs.at[mv, pl.ds(halo + span, halo)]
            to = at(leaf=me - 1)
        return remote(src, dst, halo_send.at[side], halo_recv.at[side], to)

    has = (me > 0, me < n - 1)

    spans = (pl.ds(halo, span), pl.ds(0, halo), pl.ds(halo + span, halo))

    def part(p, v):
        return vecs.at[v, spans[p]]

    def source(p):
        return vec_hbm if p == 0 else part(p, mv)

    def to_buddy(p):
        return remote(source(p), part(p, mv), vec_send.at[p, 0], vec_recv.at[p, 0], at(vec=buddy))

    def across(p, d):
        peer = ((high + d) % highs) * 2 + core
        return remote(source(p), part(p, mv), vec_send.at[p, d], vec_recv.at[p, d], at(vec=peer))

    def arrived(p, d):
        peer = ((high + highs - d) % highs) * 2 + core
        return remote(
            part(p, peer), part(p, peer), vec_send.at[p, d], vec_recv.at[p, d], at(vec=buddy)
        )

    def pass_on(p, d):
        peer = ((high + highs - d) % highs) * 2 + core
        k = highs - 1 + d
        return remote(
            part(p, peer), part(p, peer), vec_send.at[p, k], vec_recv.at[p, k], at(vec=buddy)
        )

    def from_buddy(p, d):
        other = ((high + highs - d) % highs) * 2 + 1 - core
        k = 0 if d == 0 else highs - 1 + d
        return remote(
            part(p, other), part(p, other), vec_send.at[p, k], vec_recv.at[p, k], at(vec=buddy)
        )

    def start_part(p):
        for d in range(1, highs):
            across(p, d).start()
        to_buddy(p).start()

    def forward_part(p):
        for d in range(1, highs):
            arrived(p, d).wait_recv()
            pass_on(p, d).start()

    def end_part(p):
        for d in range(highs):
            from_buddy(p, d).wait_recv()

    def end_part_sends(p):
        to_buddy(p).wait_send()
        for d in range(1, highs):
            across(p, d).wait_send()
            pass_on(p, d).wait_send()

    @pl.when(has[1])
    def _():
        halo_copy(0).start()

    @pl.when(has[0])
    def _():
        halo_copy(1).start()

    start_part(0)

    half = n // 2

    def ring_slot(direction, distance, chunk):
        origin = (pos + n - distance) % n if direction == 0 else (pos + distance) % n
        return (low_coeffs, high_coeffs)[chunk].at[pl.ds(origin * CHUNK, CHUNK)]

    def ring(direction, step, chunk, distance):
        ref = ring_slot(direction, distance, chunk)
        return remote(
            ref,
            ref,
            ring_send.at[direction, step - 1, chunk],
            ring_recv.at[direction, step - 1, chunk],
            at(leaf=nxt if direction == 0 else prv),
        )

    def has_step(direction, step, chunk):
        return 1 <= step < half or (step == half and chunk == direction)

    def ring_start(step, chunk):
        for direction in range(2):
            if has_step(direction, step, chunk):
                ring(direction, step, chunk, step - 1).start()

    def ring_turn(step, chunk):
        for direction in range(2):
            if has_step(direction, step, chunk):
                ring(direction, step, chunk, step).wait_recv()
                if has_step(direction, step + 1, chunk):
                    ring(direction, step + 1, chunk, step).start()

    base = pos * CHUNK
    loads[0].wait()
    loads[1].wait()
    leaf_coeff = []
    for i in range(leaves):
        c = dot_t(basis[i], vecs[mv, pl.ds(halo + i * LEAF, LEAF)]).astype(BF16)
        low_coeffs[base + i] = c
        leaf_coeff.append(c)
    ring_start(1, 0)
    loads[2].wait()
    loads[3].wait()
    loads[4].wait()
    mids = []
    for m in range(leaves // 2):
        c = (
            dot_t(up_leaf[2 * m], leaf_coeff[2 * m])
            + dot_t(up_leaf[2 * m + 1], leaf_coeff[2 * m + 1])
        ).astype(BF16)
        high_coeffs[base + m] = c
        mids.append(c)
    root = (dot_t(up_mid[0], mids[0]) + dot_t(up_mid[1], mids[1])).astype(BF16)
    high_coeffs[base + 2] = root
    high_coeffs[base + 3] = dot_t(top_up[0], root).astype(BF16)
    ring_start(1, 1)

    for side in range(2):
        p = side + 1

        @pl.when(has[side])
        def _():
            halo_copy(side).wait_recv()
            start_part(p)

        @pl.when(jnp.logical_not(has[side]))
        def _():
            vecs[:, spans[p]] = jnp.zeros((w, halo, width), BF16)

    forward_part(0)
    if half > 1:
        ring_turn(1, 0)
    end_part(0)

    loads[5].wait()

    def near_slot(j):
        low, top = max(0, j - NEAR + 1), min(leaves - 1, j)
        a = jnp.concatenate([near[i, j - i] for i in range(low, top + 1)], axis=0)
        b = jnp.concatenate([vecs[v, pl.ds(j * LEAF, LEAF)] for v in range(w)], axis=1)
        prod = dot(a, b)
        where = pl.ds(low * rows, (top + 1 - low) * rows)
        acc[where] += prod

    order = list(range(HALO, HALO + leaves)) + list(range(HALO)) + list(
        range(HALO + leaves, 2 * HALO + leaves)
    )
    acc[...] = jnp.zeros(acc.shape, F32)
    for j in order[:leaves]:
        near_slot(j)
    if half > 1:
        ring_turn(1, 1)
    for side in range(2):

        @pl.when(has[side])
        def _():
            forward_part(side + 1)

    if half > 2:
        ring_turn(2, 0)
    for side in range(2):

        @pl.when(has[side])
        def _():
            end_part(side + 1)

    for j in order[leaves:]:
        near_slot(j)
    for v in range(w):
        near_out[v] = acc[:, v * width : (v + 1) * width].astype(BF16)

    def back(d):
        to = (mv + d) % w
        return remote(
            near_out.at[to], near_in.at[mv], back_send.at[d], back_recv.at[d], at(vec=to)
        )

    def back_arrived(d):
        src = (mv + w - d) % w
        return remote(
            near_in.at[src], near_in.at[src], back_send.at[d], back_recv.at[d], at(vec=src)
        )

    for d in range(1, w):
        back(d).start()
    near_in[mv] = near_out[mv]
    if half > 2:
        ring_turn(2, 1)
    for step in range(3, half):
        ring_turn(step, 0)
        ring_turn(step, 1)
    ring_turn(half, 0)
    loads[6].wait()

    def far_sum(held, first, count):
        total = None
        for k in range(count):
            r = first + k
            term = dot(coup[kind_ref[r]], held[slot_ref[r]])
            total = term if total is None else total + term
        return total

    def far_leaf_step(i, _):
        far[i] = far_sum(low_coeffs, i * FAR_LEAF, FAR_LEAF)
        return _

    lax.fori_loop(0, leaves, far_leaf_step, 0)
    ring_turn(half, 1)
    loads[7].wait()
    loads[8].wait()

    def add_top(k, total):
        return total + high_coeffs[k * CHUNK + CHUNK - 1].astype(F32)

    top_coeff = lax.fori_loop(0, n, add_top, jnp.zeros((RANK, width), F32)).astype(BF16)
    top_local = dot(coup_top[...], top_coeff).astype(BF16)
    first_end = leaves * FAR_LEAF
    second_end = first_end + leaves // 2 * FAR_MID
    down_root = (far_sum(high_coeffs, second_end, FAR_ROOT) + dot(top_down[0], top_local)).astype(BF16)
    for d in range(1, w):
        back_arrived(d).wait_recv()
    for m in range(leaves // 2):
        down_mid = (
            far_sum(high_coeffs, first_end + m * FAR_MID, FAR_MID) + dot(up_mid[m], down_root)
        ).astype(BF16)
        for i in (2 * m, 2 * m + 1):
            down_leaf = (far[i] + dot(up_leaf[i], down_mid)).astype(BF16)
            field = dot(basis[i], down_leaf)
            close = jnp.concatenate(
                [near_in[u, pl.ds(i * rows, rows)] for u in range(w)], axis=0
            ).astype(F32)
            out_ref[pl.ds(i * LEAF, LEAF)] = (field + close).astype(BF16)

    end_part_sends(0)

    @pl.when(has[1])
    def _():
        halo_copy(0).wait_send()
        end_part_sends(2)

    @pl.when(has[0])
    def _():
        halo_copy(1).wait_send()
        end_part_sends(1)

    for step in range(1, half + 1):
        for chunk in range(2):
            for direction in range(2):
                if has_step(direction, step, chunk):
                    ring(direction, step, chunk, step - 1).wait_send()
    for d in range(1, w):
        back(d).wait_send()


def node_table(leaves):
    bases = np.concatenate(
        [np.zeros(leaves * FAR_LEAF), np.zeros(leaves // 2 * FAR_MID), np.full(FAR_ROOT, 2)]
    )
    moduli = np.concatenate(
        [np.full(leaves * FAR_LEAF, 4), np.full(leaves // 2 * FAR_MID, 2), np.full(FAR_ROOT, 1)]
    )
    return jnp.asarray(bases.astype(np.int32)), jnp.asarray(moduli.astype(np.int32))


def body(
    n,
    w,
    vectors,
    leaf_basis,
    up_leaf,
    up_mid,
    top_up,
    top_down,
    couplings,
    coupling_top,
    near_blocks,
    far_owner,
    far_pick,
    far_kind,
):
    device = lax.axis_index("leaf")
    span, width = vectors.shape
    leaves = leaf_basis.shape[0]
    rows = near_blocks.shape[2]
    far_rows = far_kind.shape[0]
    bases, moduli = node_table(leaves)
    owner = lax.dynamic_slice_in_dim(far_owner, device * far_rows, far_rows, 0).reshape(far_rows)
    pick = lax.dynamic_slice_in_dim(far_pick, device * far_rows, far_rows, 0)
    slots = ring_position(owner, n) * CHUNK + bases + pick % moduli
    half = n // 2
    highs = w // 2
    smem = pl.BlockSpec(memory_space=pltpu.SMEM)
    anywhere = pl.BlockSpec(memory_space=pl.ANY)
    dma = pltpu.SemaphoreType.DMA
    operands = (
        vectors,
        leaf_basis,
        up_leaf,
        up_mid,
        top_up,
        top_down,
        couplings,
        coupling_top,
        near_blocks,
    )
    return pl.pallas_call(
        functools.partial(kernel, n, w),
        out_shape=jax.ShapeDtypeStruct((span, width), BF16),
        in_specs=[smem, smem] + [anywhere] * len(operands),
        out_specs=pl.BlockSpec(memory_space=pltpu.VMEM),
        scratch_shapes=[
            pltpu.VMEM((w, span + 2 * HALO * LEAF, width), BF16),
            *[pltpu.VMEM(a.shape, BF16) for a in operands[1:]],
            pltpu.VMEM((n * CHUNK, RANK, width), BF16),
            pltpu.VMEM((n * CHUNK, RANK, width), BF16),
            pltpu.VMEM((leaves * rows, w * width), F32),
            pltpu.VMEM((leaves, RANK, width), F32),
            pltpu.VMEM((w, leaves * rows, width), BF16),
            pltpu.VMEM((w, leaves * rows, width), BF16),
            dma((9,)),
            dma((2,)),
            dma((2,)),
            dma((3, 2 * highs - 1)),
            dma((3, 2 * highs - 1)),
            dma((2, half, 2)),
            dma((2, half, 2)),
            dma((w,)),
            dma((w,)),
        ],
        compiler_params=pltpu.CompilerParams(
            collective_id=0, has_side_effects=True, vmem_limit_bytes=60 * 1024 * 1024
        ),
    )(slots, far_kind, *operands)


def solution(mesh):
    placed = (
        P("leaf", "vec"),
        P("leaf", None, None),
        P("leaf", None, None),
        P("leaf", None, None),
        P("leaf", None, None),
        P("leaf", None, None),
        P(),
        P(),
        P("leaf", None, "vec", None),
        P(),
        P(),
        P("leaf"),
    )
    return jax.shard_map(
        functools.partial(body, mesh.shape["leaf"], mesh.shape["vec"]),
        mesh=mesh,
        in_specs=placed,
        out_specs=P("leaf", "vec"),
        check_vma=False,
    )
```

```python
import functools
import jax
import jax.numpy as jnp
import numpy as np
from jax import lax
from jax.experimental import pallas as pl
from jax.experimental.pallas import tpu as pltpu
from jax.sharding import PartitionSpec as P

LEAF = 512
RANK = 256
NEAR = 5
FAR_LEAF = 8
FAR_MID = 8
FAR_ROOT = 8
HALO = NEAR // 2
CHUNKS = (4, 3)
F32 = jnp.float32
BF16 = jnp.bfloat16


def dot(a, b):
    return jnp.dot(a, b, preferred_element_type=F32)


def dot_t(a, b):
    return lax.dot_general(a, b, (((0,), (0,)), ((), ())), preferred_element_type=F32)


def ring_position(leaf, count):
    return jnp.where(leaf % 2 == 1, leaf // 2, count - 1 - leaf // 2)


def leaf_at(position, count):
    half = count // 2
    return jnp.where(position < half, 2 * position + 1, 2 * (count - 1 - position))


def kernel(
    n,
    w,
    slot_ref,
    kind_ref,
    vec_hbm,
    basis_hbm,
    up_leaf_hbm,
    up_mid_hbm,
    top_up_hbm,
    top_down_hbm,
    coup_hbm,
    coup_top_hbm,
    near_hbm,
    out_ref,
    vecs,
    basis,
    up_leaf,
    up_mid,
    top_up,
    top_down,
    coup,
    coup_top,
    near,
    low_coeffs,
    high_coeffs,
    acc,
    far,
    near_out,
    near_in,
    top_share,
    local_sem,
    halo_send,
    halo_recv,
    vec_send,
    vec_recv,
    ring_send,
    ring_recv,
    back_send,
    back_recv,
    top_send,
    top_recv,
):
    span = vec_hbm.shape[0]
    leaves = span // LEAF
    rows = near.shape[2]
    width = vec_hbm.shape[1]
    halo = HALO * LEAF
    me = lax.axis_index("leaf")
    mv = lax.axis_index("vec")
    pos = ring_position(me, n)
    nxt = leaf_at((pos + 1) % n, n)
    prv = leaf_at((pos + n - 1) % n, n)
    core, high = mv % 2, mv // 2
    highs = w // 2
    buddy = high * 2 + 1 - core

    def at(leaf=None, vec=None):
        return (me if leaf is None else leaf, mv if vec is None else vec)

    locals_ = [
        (vec_hbm, vecs.at[mv, pl.ds(halo, span)]),
        (basis_hbm, basis),
        (up_leaf_hbm, up_leaf),
        (up_mid_hbm, up_mid),
        (top_up_hbm, top_up),
        (near_hbm, near),
        (coup_hbm, coup),
        (top_down_hbm, top_down),
        (coup_top_hbm, coup_top),
    ]
    loads = [
        pltpu.make_async_copy(src, dst, local_sem.at[k]) for k, (src, dst) in enumerate(locals_)
    ]
    for load in loads:
        load.start()

    barrier = pltpu.get_barrier_semaphore()

    def greet(device):
        pl.semaphore_signal(barrier, inc=1, device_id=device, device_id_type=pl.DeviceIdType.MESH)

    greet(at(leaf=nxt))
    greet(at(leaf=prv))
    for d in range(1, w):
        greet(at(vec=(mv + d) % w))

    @pl.when(me > 0)
    def _():
        greet(at(leaf=me - 1))

    @pl.when(me < n - 1)
    def _():
        greet(at(leaf=me + 1))

    pl.semaphore_wait(
        barrier, w + 1 + (me > 0).astype(jnp.int32) + (me < n - 1).astype(jnp.int32)
    )

    def remote(src, dst, send, recv, device):
        return pltpu.make_async_remote_copy(
            src_ref=src,
            dst_ref=dst,
            send_sem=send,
            recv_sem=recv,
            device_id=device,
            device_id_type=pl.DeviceIdType.MESH,
        )

    def halo_copy(side):
        if side == 0:
            src = vec_hbm.at[pl.ds(span - halo, halo)]
            dst = vecs.at[mv, pl.ds(0, halo)]
            to = at(leaf=me + 1)
        else:
            src = vec_hbm.at[pl.ds(0, halo)]
            dst = vecs.at[mv, pl.ds(halo + span, halo)]
            to = at(leaf=me - 1)
        return remote(src, dst, halo_send.at[side], halo_recv.at[side], to)

    has = (me > 0, me < n - 1)

    spans = (pl.ds(halo, span), pl.ds(0, halo), pl.ds(halo + span, halo))

    def part(p, v):
        return vecs.at[v, spans[p]]

    def source(p):
        return vec_hbm if p == 0 else part(p, mv)

    def to_buddy(p):
        return remote(source(p), part(p, mv), vec_send.at[p, 0], vec_recv.at[p, 0], at(vec=buddy))

    def across(p, d):
        peer = ((high + d) % highs) * 2 + core
        return remote(source(p), part(p, mv), vec_send.at[p, d], vec_recv.at[p, d], at(vec=peer))

    def arrived(p, d):
        peer = ((high + highs - d) % highs) * 2 + core
        return remote(
            part(p, peer), part(p, peer), vec_send.at[p, d], vec_recv.at[p, d], at(vec=buddy)
        )

    def pass_on(p, d):
        peer = ((high + highs - d) % highs) * 2 + core
        k = highs - 1 + d
        return remote(
            part(p, peer), part(p, peer), vec_send.at[p, k], vec_recv.at[p, k], at(vec=buddy)
        )

    def from_buddy(p, d):
        other = ((high + highs - d) % highs) * 2 + 1 - core
        k = 0 if d == 0 else highs - 1 + d
        return remote(
            part(p, other), part(p, other), vec_send.at[p, k], vec_recv.at[p, k], at(vec=buddy)
        )

    def start_part(p):
        for d in range(1, highs):
            across(p, d).start()
        to_buddy(p).start()

    def forward_part(p):
        for d in range(1, highs):
            arrived(p, d).wait_recv()
            pass_on(p, d).start()

    def end_part(p):
        for d in range(highs):
            from_buddy(p, d).wait_recv()

    def end_part_sends(p):
        to_buddy(p).wait_send()
        for d in range(1, highs):
            across(p, d).wait_send()
            pass_on(p, d).wait_send()

    @pl.when(has[1])
    def _():
        halo_copy(0).start()

    @pl.when(has[0])
    def _():
        halo_copy(1).start()

    start_part(0)

    half = n // 2

    def ring_slot(direction, distance, chunk):
        origin = (pos + n - distance) % n if direction == 0 else (pos + distance) % n
        return (low_coeffs, high_coeffs)[chunk].at[
            pl.ds(origin * CHUNKS[chunk], CHUNKS[chunk])
        ]

    def ring(direction, step, chunk, distance):
        ref = ring_slot(direction, distance, chunk)
        return remote(
            ref,
            ref,
            ring_send.at[direction, step - 1, chunk],
            ring_recv.at[direction, step - 1, chunk],
            at(leaf=nxt if direction == 0 else prv),
        )

    def has_step(direction, step, chunk):
        return 1 <= step < half or (step == half and chunk == direction)

    def ring_start(step, chunk):
        for direction in range(2):
            if has_step(direction, step, chunk):
                ring(direction, step, chunk, step - 1).start()

    def ring_turn(step, chunk):
        for direction in range(2):
            if has_step(direction, step, chunk):
                ring(direction, step, chunk, step).wait_recv()
                if has_step(direction, step + 1, chunk):
                    ring(direction, step + 1, chunk, step).start()

    out, last = me // 2, half - 1

    def top_copy(src, dst, to):
        return remote(
            top_share.at[src], top_share.at[dst], top_send.at[dst], top_recv.at[dst], at(leaf=to)
        )

    def top_pair():
        return top_share[0].astype(F32) + top_share[1].astype(F32)

    def top_point(t):
        if t == 0:
            top_copy(0, 1, me + 1 - 2 * (me % 2)).wait_recv()

        @pl.when(out == t)
        def _():
            if t == 0:
                top_share[4] = jnp.zeros((RANK, width), BF16)
            else:
                top_copy(2, 4, me + 2).wait_recv()
            top_share[2] = (top_pair() + top_share[4].astype(F32)).astype(BF16)
            top_copy(2, 4, me + 2).start()

        @pl.when(out == last - t)
        def _():
            if t == 0:
                top_share[5] = jnp.zeros((RANK, width), BF16)
            else:
                top_copy(3, 5, me - 2).wait_recv()
            top_share[3] = (top_pair() + top_share[5].astype(F32)).astype(BF16)
            top_copy(3, 5, me - 2).start()

    base, high_base = pos * CHUNKS[0], pos * CHUNKS[1]
    loads[0].wait()
    loads[1].wait()
    leaf_coeff = []
    for i in range(leaves):
        c = dot_t(basis[i], vecs[mv, pl.ds(halo + i * LEAF, LEAF)]).astype(BF16)
        low_coeffs[base + i] = c
        leaf_coeff.append(c)
    ring_start(1, 0)
    loads[2].wait()
    loads[3].wait()
    loads[4].wait()
    mids = []
    for m in range(leaves // 2):
        c = (
            dot_t(up_leaf[2 * m], leaf_coeff[2 * m])
            + dot_t(up_leaf[2 * m + 1], leaf_coeff[2 * m + 1])
        ).astype(BF16)
        high_coeffs[high_base + m] = c
        mids.append(c)
    root = (dot_t(up_mid[0], mids[0]) + dot_t(up_mid[1], mids[1])).astype(BF16)
    high_coeffs[high_base + 2] = root
    top_share[0] = dot_t(top_up[0], root).astype(BF16)
    top_copy(0, 1, me + 1 - 2 * (me % 2)).start()
    ring_start(1, 1)

    for side in range(2):
        p = side + 1

        @pl.when(has[side])
        def _():
            halo_copy(side).wait_recv()
            start_part(p)

        @pl.when(jnp.logical_not(has[side]))
        def _():
            vecs[:, spans[p]] = jnp.zeros((w, halo, width), BF16)

    forward_part(0)
    if half > 1:
        ring_turn(1, 0)
        top_point(0)
    end_part(0)

    loads[5].wait()

    def near_slot(j):
        low, top = max(0, j - NEAR + 1), min(leaves - 1, j)
        a = jnp.concatenate([near[i, j - i] for i in range(low, top + 1)], axis=0)
        b = jnp.concatenate([vecs[v, pl.ds(j * LEAF, LEAF)] for v in range(w)], axis=1)
        prod = dot(a, b)
        where = pl.ds(low * rows, (top + 1 - low) * rows)
        acc[where] += prod

    order = list(range(HALO, HALO + leaves)) + list(range(HALO)) + list(
        range(HALO + leaves, 2 * HALO + leaves)
    )
    acc[...] = jnp.zeros(acc.shape, F32)
    for j in order[:leaves]:
        near_slot(j)
    if half > 1:
        ring_turn(1, 1)
    if last > 1:
        top_point(1)
    for side in range(2):

        @pl.when(has[side])
        def _():
            forward_part(side + 1)

    if half > 2:
        ring_turn(2, 0)
    for side in range(2):

        @pl.when(has[side])
        def _():
            end_part(side + 1)

    for j in order[leaves:]:
        near_slot(j)
    for v in range(w):
        near_out[v] = acc[:, v * width : (v + 1) * width].astype(BF16)

    def back(d):
        to = (mv + d) % w
        return remote(
            near_out.at[to], near_in.at[mv], back_send.at[d], back_recv.at[d], at(vec=to)
        )

    def back_arrived(d):
        src = (mv + w - d) % w
        return remote(
            near_in.at[src], near_in.at[src], back_send.at[d], back_recv.at[d], at(vec=src)
        )

    for d in range(1, w):
        back(d).start()
    near_in[mv] = near_out[mv]
    if half > 2:
        ring_turn(2, 1)
    for t in range(2, last):
        top_point(t)
    for step in range(3, half):
        ring_turn(step, 0)
        ring_turn(step, 1)
    ring_turn(half, 0)
    loads[6].wait()

    def far_sum(held, first, count):
        total = None
        for k in range(count):
            r = first + k
            term = dot(coup[kind_ref[r]], held[slot_ref[r]])
            total = term if total is None else total + term
        return total

    def far_leaf_step(i, _):
        far[i] = far_sum(low_coeffs, i * FAR_LEAF, FAR_LEAF)
        return _

    lax.fori_loop(0, leaves, far_leaf_step, 0)
    ring_turn(half, 1)
    loads[7].wait()
    loads[8].wait()

    @pl.when(out == last)
    def _():
        top_copy(2, 4, me - 2).wait_recv()

    @pl.when(out == 0)
    def _():
        top_copy(3, 5, me + 2).wait_recv()

    top_coeff = (top_pair() + top_share[4].astype(F32) + top_share[5].astype(F32)).astype(BF16)
    top_local = dot(coup_top[...], top_coeff).astype(BF16)
    first_end = leaves * FAR_LEAF
    second_end = first_end + leaves // 2 * FAR_MID
    down_root = (far_sum(high_coeffs, second_end, FAR_ROOT) + dot(top_down[0], top_local)).astype(BF16)
    for d in range(1, w):
        back_arrived(d).wait_recv()
    for m in range(leaves // 2):
        down_mid = (
            far_sum(high_coeffs, first_end + m * FAR_MID, FAR_MID) + dot(up_mid[m], down_root)
        ).astype(BF16)
        for i in (2 * m, 2 * m + 1):
            down_leaf = (far[i] + dot(up_leaf[i], down_mid)).astype(BF16)
            field = dot(basis[i], down_leaf)
            close = jnp.concatenate(
                [near_in[u, pl.ds(i * rows, rows)] for u in range(w)], axis=0
            ).astype(F32)
            out_ref[pl.ds(i * LEAF, LEAF)] = (field + close).astype(BF16)

    end_part_sends(0)

    @pl.when(has[1])
    def _():
        halo_copy(0).wait_send()
        end_part_sends(2)

    @pl.when(has[0])
    def _():
        halo_copy(1).wait_send()
        end_part_sends(1)

    for step in range(1, half + 1):
        for chunk in range(2):
            for direction in range(2):
                if has_step(direction, step, chunk):
                    ring(direction, step, chunk, step - 1).wait_send()
    for d in range(1, w):
        back(d).wait_send()
    top_copy(0, 1, me + 1 - 2 * (me % 2)).wait_send()

    @pl.when(out < last)
    def _():
        top_copy(2, 4, me + 2).wait_send()

    @pl.when(out > 0)
    def _():
        top_copy(3, 5, me - 2).wait_send()


def node_table(leaves):
    bases = np.concatenate(
        [np.zeros(leaves * FAR_LEAF), np.zeros(leaves // 2 * FAR_MID), np.full(FAR_ROOT, 2)]
    )
    moduli = np.concatenate(
        [np.full(leaves * FAR_LEAF, 4), np.full(leaves // 2 * FAR_MID, 2), np.full(FAR_ROOT, 1)]
    )
    return jnp.asarray(bases.astype(np.int32)), jnp.asarray(moduli.astype(np.int32))


def body(
    n,
    w,
    vectors,
    leaf_basis,
    up_leaf,
    up_mid,
    top_up,
    top_down,
    couplings,
    coupling_top,
    near_blocks,
    far_owner,
    far_pick,
    far_kind,
):
    device = lax.axis_index("leaf")
    span, width = vectors.shape
    leaves = leaf_basis.shape[0]
    rows = near_blocks.shape[2]
    far_rows = far_kind.shape[0]
    bases, moduli = node_table(leaves)
    owner = lax.dynamic_slice_in_dim(far_owner, device * far_rows, far_rows, 0).reshape(far_rows)
    pick = lax.dynamic_slice_in_dim(far_pick, device * far_rows, far_rows, 0)
    strides = np.full(far_rows, CHUNKS[1], np.int32)
    strides[: leaves * FAR_LEAF] = CHUNKS[0]
    slots = ring_position(owner, n) * strides + bases + pick % moduli
    half = n // 2
    highs = w // 2
    smem = pl.BlockSpec(memory_space=pltpu.SMEM)
    anywhere = pl.BlockSpec(memory_space=pl.ANY)
    dma = pltpu.SemaphoreType.DMA
    operands = (
        vectors,
        leaf_basis,
        up_leaf,
        up_mid,
        top_up,
        top_down,
        couplings,
        coupling_top,
        near_blocks,
    )
    return pl.pallas_call(
        functools.partial(kernel, n, w),
        out_shape=jax.ShapeDtypeStruct((span, width), BF16),
        in_specs=[smem, smem] + [anywhere] * len(operands),
        out_specs=pl.BlockSpec(memory_space=pltpu.VMEM),
        scratch_shapes=[
            pltpu.VMEM((w, span + 2 * HALO * LEAF, width), BF16),
            *[pltpu.VMEM(a.shape, BF16) for a in operands[1:]],
            *[pltpu.VMEM((n * c, RANK, width), BF16) for c in CHUNKS],
            pltpu.VMEM((leaves * rows, w * width), F32),
            pltpu.VMEM((leaves, RANK, width), F32),
            pltpu.VMEM((w, leaves * rows, width), BF16),
            pltpu.VMEM((w, leaves * rows, width), BF16),
            pltpu.VMEM((6, RANK, width), BF16),
            dma((9,)),
            dma((2,)),
            dma((2,)),
            dma((3, 2 * highs - 1)),
            dma((3, 2 * highs - 1)),
            dma((2, half, 2)),
            dma((2, half, 2)),
            dma((w,)),
            dma((w,)),
            dma((6,)),
            dma((6,)),
        ],
        compiler_params=pltpu.CompilerParams(
            collective_id=0, has_side_effects=True, vmem_limit_bytes=60 * 1024 * 1024
        ),
    )(slots, far_kind, *operands)


def solution(mesh):
    placed = (
        P("leaf", "vec"),
        P("leaf", None, None),
        P("leaf", None, None),
        P("leaf", None, None),
        P("leaf", None, None),
        P("leaf", None, None),
        P(),
        P(),
        P("leaf", None, "vec", None),
        P(),
        P(),
        P("leaf"),
    )
    return jax.shard_map(
        functools.partial(body, mesh.shape["leaf"], mesh.shape["vec"]),
        mesh=mesh,
        in_specs=placed,
        out_specs=P("leaf", "vec"),
        check_vma=False,
    )
```
